512 devices in a mesh: users: 32 (over z, core), hist: 16 (over x, y).
Axes of the slice: x: 4, y: 4, z: 16, core: 2. Of those that a mesh axis runs over, the one named last changes fastest.
Arguments:
- item_table: bfloat16 [8192, 1024], P('users'), may hold values from -40 to 40
- cand_owner: int32 [32, 768, 1], P('users', 'hist'), may hold values from 0 to 31; in each aligned block of 48 rows (0 to 47, 48 to 95, ..., all dimensions but the last counted through in order) at most 3 rows name the same one
- cand_row: int32 [32, 768], P('users', 'hist'), may hold values from 0 to 255
- counts: int32 [32], P('users'), may hold values from 1 to 768, 15360 in all
- hist_keys: bfloat16 [32, 8192, 1024], P('users', 'hist'), may hold values from -6 to 6
- hist_values: bfloat16 [32, 8192, 1024], P('users', 'hist'), may hold values from -25 to 25
- gain_in: float32 [1024], replicated, may hold values from 0.25 to 1.75
- w_in: bfloat16 [1024, 2048], P('hist'), may hold values from -0.1875 to 0.1875
- bias_in: float32 [2048], replicated, may hold values from -3 to 3
- gain_mid: float32 [1024], replicated, may hold values from 0.25 to 1.75
- w_out: bfloat16 [1024, 1024], P('hist'), may hold values from -0.1875 to 0.1875
Outputs:
- ranked: bfloat16 [32, 768, 1024], P('users', 'hist')
The draws below stay inside these ranges and needn't reach their ends.
Inputs may be any that keep to these rules, and one draw needn't show every extreme that they name: `cand_owner`: in each aligned block of 48 candidates (the candidates of one device), no table shard is named more than 3 times, and one shard exactly 3 times in some blocks. The live candidates of a user are its first counts[u] slots; some user has all 768.
All inputs are finite; a program needn't handle non-finite values. No bound on the sum of `counts` on one device may be relied on, other than what follows from the above.
Results may differ from the reference program's by a relative error of at most 0.0045.
Values may be sent and summed in bfloat16 or wider, within the bound.
A program may use at most 64 MiB of HBM per device.

```python
import math
import jax
import jax.numpy as jnp
import numpy as np
from jax import lax

D = 1024
HEADS = 8
CAND_DEV = 48
ROWS_DEV = 256
USERS = 32
HIST = 8192
CAND = 768
ITEMS = 8192
SLOT = 3
N_USERS = 32


def draw_item_table(key, part):
    key = jax.random.fold_in(key, 7)
    base_key, row_key, col_key = jax.random.split(key, 3)
    row_scale = jnp.exp(jax.random.uniform(row_key, (ITEMS, 1), jnp.float32, math.log(0.3), math.log(3.0)))
    col_scale = jnp.exp(jax.random.uniform(col_key, (1, D), jnp.float32, math.log(0.3), math.log(3.0)))
    base = jax.random.truncated_normal(base_key, -4.0, 4.0, (ITEMS, D), jnp.float32)
    return (base * row_scale * col_scale).astype(jnp.bfloat16)


def draw_hist_values(key, part):
    key = jax.random.fold_in(key, 13)
    base_key = jax.random.fold_in(key, 0)
    col_key = jax.random.fold_in(key, 2)
    col_scale = 0.5 * jnp.exp(jax.random.uniform(col_key, (1, 1, D), jnp.float32, 0.0, math.log(10.0)))
    base = jax.random.truncated_normal(base_key, -4.0, 4.0, (USERS, HIST, D), jnp.float32)
    return (base * col_scale).astype(jnp.bfloat16)


def place_ends(array, stream_key, least, high):
    longest = array.shape.index(max(array.shape))
    spots = []
    for shift in (0, 1):
        where = [jax.random.randint(jax.random.fold_in(stream_key, axis), (), 0, length) for axis, length in enumerate(array.shape)]
        where[longest] = (where[longest] + shift) % array.shape[longest]
        spots.append(tuple(where))
    return array.at[spots[0]].set(least).at[spots[1]].set(high)


def steps_of(key, extent, shards, least, top_value):
    def one(position, parts):
        steps = jax.random.uniform(jax.random.fold_in(jax.random.fold_in(key, 6), position), (parts,), jnp.float32, least / len(shards), top_value / len(shards))
        return jnp.repeat(jnp.exp(steps), extent[position] // parts).reshape((-1,) + (1,) * (len(extent) - position - 1))

    factor_of = one(*shards[0])
    for cut in shards[1:]:
        factor_of = factor_of * one(*cut)
    return factor_of


def split_up(amount, total, reach, slope):
    weights = [(1 << 20) // math.isqrt(standing ** slope) + 1 for standing in range(2, amount + 1)]
    spare, given = total - reach - (amount - 1), [1] * (amount - 1)
    while spare > 0:
        free = [i for i in range(amount - 1) if given[i] < reach]
        whole, left = sum([weights[i] for i in free]), spare
        for i in free:
            more = min(reach - given[i], max(1, left * weights[i] // whole), spare)
            given[i] = given[i] + more
            spare = spare - more
    return np.array([reach] + given)


def ragged(key, count, total, limit, skew):
    if count == 2:
        one = jax.random.randint(key, (), max(1, total - limit), min(limit, total - 1) + 1)
        return jnp.stack([one, total - one])
    sizes = jnp.asarray(split_up(count, total, limit, skew), jnp.int32)
    couples = (count - 1) // 2
    donor, sink = sizes[1:1 + 2 * couples:2], sizes[2:2 + 2 * couples:2]
    margin = jnp.minimum(donor - 1, limit - sink)
    shifted = jax.random.randint(jax.random.fold_in(key, 1), (couples,), 0, 1 << 20) % (margin + 1)
    sizes = sizes.at[1:1 + 2 * couples:2].set(donor - shifted).at[2:2 + 2 * couples:2].set(sink + shifted)
    return sizes[jax.random.permutation(jax.random.fold_in(key, 2), count)]


def deal_out(key, own, number, rows, number_of, top, most, lean):
    ranking = jax.random.permutation(key, number_of)
    heavy_load, usual = load_shares(number_of, rows * top, most, lean, True), load_shares(number_of, rows * top, most, lean, False)
    places = jnp.arange(number_of)

    def named(sizes, rotation):
        used = int((sizes > 0).sum())
        fixed = max(1, used // 4)
        shifted = fixed + (places - fixed + rotation * (used - fixed)) % max(1, number_of - fixed)
        return jnp.zeros((number_of,), jnp.int32).at[ranking[jnp.where(places < fixed, places, shifted)]].set(jnp.asarray(sizes, jnp.int32))

    sizes = jnp.where(number % 4 == 0, named(heavy_load, number // 4), named(usual, number - number // 4 - 1))
    mixed = jax.random.permutation(jax.random.fold_in(own, 3), number_of)
    donor, sink = mixed[0:number_of // 2 * 2:2], mixed[1:number_of // 2 * 2:2]
    slack = jnp.minimum(sizes[donor] - 1, most - sizes[sink]) // 2
    slack = jnp.where((donor == ranking[0]) | (sink == ranking[0]) | (sizes[sink] == 0), 0, jnp.maximum(slack, 0))
    shifted = jax.random.randint(jax.random.fold_in(own, 4), (number_of // 2,), 0, 1 << 20) % (slack + 1)
    sizes = sizes.at[donor].add(-shifted).at[sink].add(shifted)
    labels = jnp.searchsorted(jnp.cumsum(sizes), jnp.arange(rows * top), side="right").astype(jnp.int32)
    table = labels.reshape(top, rows).T
    table = table[jax.random.permutation(jax.random.fold_in(own, 1), rows)]
    rotation = jax.random.randint(jax.random.fold_in(own, 2), (rows, 1), 0, top)
    return jnp.take_along_axis(table, (jnp.arange(top)[None, :] + rotation) % top, axis=1)


def load_shares(count, total, most, slope, full):
    loads = [(1 << 20) // math.isqrt(standing ** slope) + 1 for standing in range(1, count + 1)]
    largest = most if full else min(most, max(-(-total // count), total * loads[0] // sum(loads)))
    least = 1 if total - largest >= count - 1 else 0
    holding, surplus = [largest] + [least] * (count - 1), total - largest - least * (count - 1)
    while surplus > 0:
        free = [i for i in range(1, count) if holding[i] < largest] or [i for i in range(1, count) if holding[i] < most]
        mass, remaining = sum([loads[i] for i in free]), surplus
        for i in free:
            extra = min(most - holding[i], max(1, remaining * loads[i] // mass), surplus)
            holding[i] = holding[i] + extra
            surplus = surplus - extra
    return np.array(holding)


def gaussian(own_key, extent, width, most, pieces=(), kind=jnp.bfloat16):
    level = steps_of(own_key, extent, pieces, -0.22, 0.18) if pieces else 1.0
    drawn = jax.random.normal(own_key, extent, jnp.float32) * width * level
    return jnp.minimum(jnp.maximum(drawn, -most), most).astype(kind)


def setup_inputs(seed: int = 0) -> dict:
    arg_keys = jax.random.split(jax.random.key(seed), 12)
    item_table = draw_item_table(jax.random.fold_in(arg_keys[11], 71), 0)
    cand_owner_keys = jax.random.split(jax.random.fold_in(arg_keys[1], 1), USERS * CAND // CAND_DEV)
    cand_owner_turns = jax.random.permutation(jax.random.fold_in(arg_keys[1], 3), USERS * CAND // CAND_DEV)
    cand_owner = jax.vmap(lambda own, number: deal_out(jax.random.fold_in(arg_keys[1], 2), own, number, CAND_DEV, N_USERS, 1, SLOT, 2))(cand_owner_keys, cand_owner_turns).reshape((USERS, CAND, 1))
    cand_row = place_ends(jax.random.randint(arg_keys[2], (USERS, CAND), 0, ROWS_DEV), jax.random.fold_in(arg_keys[2], 1), 0, ROWS_DEV - 1).astype(jnp.int32)
    counts = ragged(arg_keys[3], USERS, USERS * CAND * 5 // 8, CAND, 2).astype(jnp.int32)
    hist_keys = gaussian(arg_keys[4], (USERS, HIST, D), 1.0, 6.0, ((0, 32), (1, 16)))
    hist_values = draw_hist_values(jax.random.fold_in(arg_keys[11], 71), 0)
    gain_in = jnp.clip(1.0 + 0.15 * jax.random.normal(arg_keys[6], (D,), jnp.float32), 0.25, 1.75)
    w_in = gaussian(arg_keys[7], (D, 2 * D), D ** -0.5, 0.1875, ((0, 16),))
    bias_in = gaussian(arg_keys[8], (2 * D,), 0.5, 3.0, (), jnp.float32)
    gain_mid = jnp.clip(1.0 + 0.15 * jax.random.normal(arg_keys[9], (D,), jnp.float32), 0.25, 1.75)
    w_out = gaussian(arg_keys[10], (D, D), D ** -0.5, 0.1875, ((0, 16),))
    return {"item_table": item_table, "cand_owner": cand_owner, "cand_row": cand_row, "counts": counts, "hist_keys": hist_keys, "hist_values": hist_values, "gain_in": gain_in, "w_in": w_in, "bias_in": bias_in, "gain_mid": gain_mid, "w_out": w_out}


eps = 1e-05

def layer_norm(values, gain):
    mean = lax.optimization_barrier(jnp.mean(values, axis=-1, keepdims=True))
    centred = values - mean
    spread = lax.optimization_barrier(jnp.mean(centred * centred, axis=-1, keepdims=True))
    return centred * lax.rsqrt(spread + eps) * gain

def reference(item_table, cand_owner, cand_row, counts, hist_keys, hist_values, gain_in, w_in, bias_in, gain_mid, w_out):
    head_size = D // HEADS

    def one_user(inputs):
        owners, rows_local, live, keys, values = inputs
        ident = (owners[:, 0] * ROWS_DEV + rows_local).astype(jnp.int32)
        fetched = jnp.take(item_table, ident, axis=0)
        normed = layer_norm(fetched.astype(jnp.float32), gain_in).astype(jnp.bfloat16)
        activated = jax.nn.silu(jnp.dot(normed, w_in, preferred_element_type=jnp.float32) + bias_in).astype(jnp.bfloat16)
        gate_rows = activated[:, :D]
        queries = activated[:, D:]
        outputs = []
        for head_index in range(HEADS):
            first = head_index * head_size
            scores = jnp.dot(queries[:, first:first + head_size], keys[:, first:first + head_size].T, preferred_element_type=jnp.float32) * head_size ** (-0.5)
            weights = jax.nn.silu(scores).astype(jnp.bfloat16)
            outputs.append(jnp.dot(weights, values[:, first:first + head_size], preferred_element_type=jnp.float32))
        attended = jnp.concatenate(outputs, axis=1)
        gated = (layer_norm(attended, gain_mid) * gate_rows.astype(jnp.float32)).astype(jnp.bfloat16)
        mixed = jnp.dot(gated, w_out, preferred_element_type=jnp.float32) + fetched.astype(jnp.float32)
        alive = jnp.arange(CAND) < live
        return jnp.where(alive[:, None], mixed, 0.0).astype(jnp.bfloat16)
    return lax.map(one_user, (cand_owner, cand_row, counts, hist_keys, hist_values))
```

```python
import functools

import jax
import jax.numpy as jnp
from jax import lax
from jax.experimental import pallas as pl
from jax.experimental.pallas import tpu as pltpu
from jax.sharding import PartitionSpec as P

MESH = pl.DeviceIdType.MESH
F32, BF16 = jnp.float32, jnp.bfloat16

HEADS = 8
HEAD = 128
D = 1024
HALF = D // 2
QUARTER = D // 4
CAND = 48
ROWS = 256
PLANES = 16
SIDE = 4
SHARD = D // (SIDE * SIDE)
SLOTS = 6
PIECES = 8
MESSAGE = SLOTS * PIECES
EPS = 1e-05
MESSAGES = 160

GROUPS = ((1, 15, 2, 14), (3, 13, 4, 12), (5, 11, 6, 10), (7, 9, 8, 0))


def norm(values, gain):
    mean = jnp.mean(values, axis=-1, keepdims=True)
    centred = values - mean
    spread = jnp.mean(centred * centred, axis=-1, keepdims=True)
    return centred * lax.rsqrt(spread + EPS) * gain


def silu(values):
    half = values * 0.5
    return half + half * jnp.tanh(half)


def kernel(
    table_ref,
    owner_row_ref,
    row_row_ref,
    counts_ref,
    keys_ref,
    values_ref,
    gain_in_ref,
    w_in_ref,
    bias_ref,
    gain_mid_ref,
    w_out_ref,
    out_ref,
    table,
    keys,
    values,
    wq,
    wr,
    plan,
    asked,
    served,
    rows,
    fetched,
    normed,
    gates,
    queries,
    own,
    part_out,
    part_in,
    sum_out,
    sum_in,
    send_sem,
    recv_sem,
    local_sem,
):
    users, hist = lax.axis_index("users"), lax.axis_index("hist")
    z, c = users // 2, lax.rem(users, 2)
    x, y = hist // SIDE, lax.rem(hist, SIDE)

    def at_z(step):
        return (lax.rem(z + step, PLANES) * 2 + c, hist)

    def at_axis(axis, step):
        if axis == "x":
            return (users, lax.rem(x + step, SIDE) * SIDE + y)
        return (users, x * SIDE + lax.rem(y + step, SIDE))

    partner = (z * 2 + 1 - c, hist)
    started = []

    def send(src, dst, device):
        index = len(started)
        copy = pltpu.make_async_remote_copy(
            src_ref=src,
            dst_ref=dst,
            send_sem=send_sem.at[index],
            recv_sem=recv_sem.at[index],
            device_id=device,
            device_id_type=MESH,
        )
        copy.start()
        started.append(copy)
        return copy

    barrier = pltpu.get_barrier_semaphore()
    peers = [at_z(step) for step in range(1, PLANES)] + [partner]
    peers += [at_axis(axis, step) for axis in "xy" for step in range(1, SIDE)]
    for peer in peers:
        pl.semaphore_signal(barrier, inc=1, device_id=peer, device_id_type=MESH)

    locals_ = []

    def load(src, dst):
        copy = pltpu.make_async_copy(src, dst, local_sem.at[len(locals_)])
        copy.start()
        locals_.append(copy)
        return copy

    load_q, load_r = [], []
    for core in range(2):
        for half in range(2):
            first = (core * 2 + half) * QUARTER
            load_q.append(load(w_in_ref.at[:, pl.ds(D + first, QUARTER)], wq.at[core, half, x, y]))
    load_table = load(table_ref, table.at[c])
    for core in range(2):
        for half in range(2):
            first = (core * 2 + half) * QUARTER
            mine = wr.at[core, half, x, y]
            load_r.append(load(w_in_ref.at[:, pl.ds(first, QUARTER)], mine.at[:, pl.ds(0, QUARTER)]))
            load_r.append(
                load(w_out_ref.at[:, pl.ds(first, QUARTER)], mine.at[:, pl.ds(QUARTER, QUARTER)])
            )
    load_keys = load(keys_ref, keys)
    load_values = load(values_ref, values)

    chip_row = ((owner_row_ref[...] >> 1) - z) & (PLANES - 1)
    later = lax.broadcasted_iota(jnp.int32, (CAND, CAND), 0)
    earlier = lax.broadcasted_iota(jnp.int32, (CAND, CAND), 1)
    chip_col = jnp.where(earlier == later, chip_row.astype(F32), 0.0)
    chip_col = jnp.sum(chip_col, axis=1, keepdims=True).astype(jnp.int32)
    before = earlier < later
    same = jnp.where((chip_col == chip_row) & before, 1.0, 0.0)
    rank = jnp.sum(same, axis=1, keepdims=True).astype(jnp.int32)
    lane = lax.broadcasted_iota(jnp.int32, (CAND, 128), 1) & 63
    slot_of = jnp.where((lane >> 3 == rank) & (lane < MESSAGE), 1.0, 0.0).astype(BF16)
    chip_of = chip_row == lax.broadcasted_iota(jnp.int32, (PLANES, CAND), 0)
    row_part = jnp.where(chip_of, row_row_ref[...].astype(F32), 0.0).astype(BF16)
    core_part = jnp.where(chip_of, ((owner_row_ref[...] & 1) + 1).astype(F32), 0.0).astype(BF16)
    wanted = jnp.dot(row_part, slot_of, preferred_element_type=F32)
    wanted += (jnp.dot(core_part, slot_of, preferred_element_type=F32) - 1.0) * ROWS
    wanted = wanted.astype(jnp.int32)
    for step in range(PLANES):
        plan[step] = wanted[step : step + 1]
    asked[0] = wanted[0:1]

    for copy in load_q:
        copy.wait()
    pl.semaphore_wait(barrier, len(peers))

    share_table = send(table_ref, table.at[c], partner)
    asks = {}
    for step in (8, 7, 9, 6, 10, 5, 11, 4, 12, 3, 13, 2, 14, 1, 15):
        asks[PLANES - step] = send(plan.at[step], asked.at[PLANES - step], at_z(step))

    axes = (("y", "x"), ("x", "y"))

    def block(buffer, half, outer, inner):
        if half == 0:
            return buffer.at[c, 0, lax.rem(x + outer, SIDE), lax.rem(y + inner, SIDE)]
        return buffer.at[c, 1, lax.rem(x + inner, SIDE), lax.rem(y + outer, SIDE)]

    def group(buffer, half, outer, first, count):
        if half == 0:
            return buffer.at[c, 0, lax.rem(x + outer, SIDE), pl.ds(first, count)]
        return buffer.at[c, 1, pl.ds(first, count), lax.rem(y + outer, SIDE)]

    def weight_inner(buffer, half):
        mine = block(buffer, half, 0, 0)
        return [send(mine, mine, at_axis(axes[half][0], step)) for step in (2, 1, 3)]

    def weight_outer(buffer, half):
        low, high = group(buffer, half, 0, 0, 2), group(buffer, half, 0, 2, 2)
        axis = axes[half][1]
        return {
            "low_up": send(low, low, at_axis(axis, 1)),
            "high_down": send(high, high, at_axis(axis, 3)),
            "high_up": send(high, high, at_axis(axis, 1)),
            "low_down": send(low, low, at_axis(axis, 3)),
        }

    def weight_relay(buffer, half, first_hop):
        axis = axes[half][1]
        first_hop["low_up"].wait_recv()
        low = group(buffer, half, 3, 0, 2)
        up = send(low, low, at_axis(axis, 1))
        first_hop["high_down"].wait_recv()
        high = group(buffer, half, 1, 2, 2)
        return up, send(high, high, at_axis(axis, 3))

    def share(ref):
        return send(ref, ref, partner)

    shared_q, shared_r = [], []
    inner_q = [weight_inner(wq, half) for half in range(2)]
    for half in range(2):
        for copy in inner_q[half]:
            copy.wait_recv()
    outer_q = [weight_outer(wq, half) for half in range(2)]
    for copy in load_r:
        copy.wait()
    inner_r = [weight_inner(wr, half) for half in range(2)]
    for half in range(2):
        shared_q += [share(block(wq, half, 0, inner)) for inner in range(1, SIDE)]

    load_table.wait()
    share_table.wait_recv()
    lanes = lax.broadcasted_iota(jnp.int32, (1, 128), 1)
    items = lax.broadcasted_iota(jnp.int32, (2 * ROWS, 128), 0)
    answers = {}

    def serve(index):
        steps = GROUPS[index]
        for step in steps:
            if step:
                asks[step].wait_recv()
        picks = []
        for pair in (steps[:2], steps[2:]):
            want = jnp.where(lanes < 64, asked[pair[0]], asked[pair[1]])
            picks.append(jnp.where(items == want, 1.0, 0.0).astype(BF16))
        found = lax.dot_general(
            jnp.concatenate(picks, axis=1),
            table[...].reshape(2 * ROWS, D),
            (((0,), (0,)), ((), ())),
            preferred_element_type=F32,
        )
        piece = lax.broadcasted_iota(jnp.int32, (256, 128), 0) & (PIECES - 1)
        packed = jnp.zeros((256, 128), F32)
        for j in range(PIECES):
            packed = jnp.where(piece == j, found[:, j * 128 : (j + 1) * 128], packed)
        served[index] = packed.astype(BF16)
        for place, step in enumerate(steps):
            if step:
                answers[PLANES - step] = send(
                    served.at[index, pl.ds(place * 64, MESSAGE)],
                    rows.at[PLANES - step],
                    at_z(step),
                )
            else:
                rows[0] = packed[place * 64 : place * 64 + MESSAGE].astype(BF16)

    for index in range(len(GROUPS)):
        serve(index)

    relay_q = [weight_relay(wq, half, outer_q[half]) for half in range(2)]
    for half in range(2):
        for copy in inner_r[half]:
            copy.wait_recv()
    outer_r = [weight_outer(wr, half) for half in range(2)]

    def weight_finish(buffer, half, first_hop, relayed, shared):
        first_hop["high_up"].wait_recv()
        shared.append(share(group(buffer, half, 3, 0, SIDE)))
        first_hop["low_down"].wait_recv()
        shared.append(share(group(buffer, half, 1, 0, SIDE)))
        for copy in relayed:
            copy.wait_recv()
        shared.append(share(group(buffer, half, 2, 0, SIDE)))

    for half in range(2):
        weight_finish(wq, half, outer_q[half], relay_q[half], shared_q)
    for half in range(2):
        shared_r += [share(block(wr, half, 0, inner)) for inner in range(1, SIDE)]

    for step in range(1, PLANES):
        answers[step].wait_recv()
    place = chip_col * MESSAGE + rank * PIECES
    column = lax.broadcasted_iota(jnp.int32, (CAND, PLANES * MESSAGE), 1)
    picks = jnp.concatenate(
        [jnp.where(column == place + j, 1.0, 0.0).astype(BF16) for j in range(PIECES)], axis=0
    )
    found = jnp.dot(picks, rows[...].reshape(PLANES * MESSAGE, 128), preferred_element_type=F32)
    for j in range(PIECES):
        fetched[:, j * 128 : (j + 1) * 128] = found[j * CAND : (j + 1) * CAND].astype(BF16)
    normed[...] = norm(fetched[...].astype(F32), gain_in_ref[...]).astype(BF16)

    relay_r = [weight_relay(wr, half, outer_r[half]) for half in range(2)]

    for copy in shared_q:
        copy.wait_recv()
    for core in range(2):
        for half in range(2):
            first = (core * 2 + half) * QUARTER
            projected = jnp.dot(
                normed[...], wq[core, half].reshape(D, QUARTER), preferred_element_type=F32
            )
            active = silu(projected + bias_ref[:, D + first : D + first + QUARTER])
            queries[core, 0, 0, :, half * QUARTER : (half + 1) * QUARTER] = active.astype(BF16)

    inner = []
    for half in range(2):
        mine = queries.at[half, 0, 0]
        inner.append(
            [
                send(mine, queries.at[half, 0, SIDE - step], at_axis(axes[half][0], step))
                for step in (2, 1, 3)
            ]
        )
    outer = []
    for half in range(2):
        for copy in inner[half]:
            copy.wait_recv()
        axis = axes[half][1]
        low, high = queries.at[half, 0, pl.ds(0, 2)], queries.at[half, 0, pl.ds(2, 2)]
        outer.append(
            {
                "low_up": send(low, queries.at[half, 3, pl.ds(0, 2)], at_axis(axis, 1)),
                "high_down": send(high, queries.at[half, 1, pl.ds(2, 2)], at_axis(axis, 3)),
                "high_up": send(high, queries.at[half, 3, pl.ds(2, 2)], at_axis(axis, 1)),
                "low_down": send(low, queries.at[half, 1, pl.ds(0, 2)], at_axis(axis, 3)),
            }
        )

    load_keys.wait()
    load_values.wait()

    def attend(half, step, target):
        for head in range(HEADS // 2):
            there = slice(head * HEAD, (head + 1) * HEAD)
            first = half * HALF + head * HEAD
            query = queries[half, step, :, :, there].reshape(SIDE * CAND, HEAD)
            scores = lax.dot_general(
                query,
                keys[:, first : first + HEAD],
                (((1,), (1,)), ((), ())),
                preferred_element_type=F32,
            )
            weights = silu(scores * HEAD**-0.5).astype(BF16)
            total = jnp.dot(weights, values[:, first : first + HEAD], preferred_element_type=F32)
            target[:, :, there] = total.reshape(SIDE, CAND, HEAD).astype(target.dtype)

    for half in range(2):
        attend(half, 0, own.at[half])

    relay = []
    for half in range(2):
        axis = axes[half][1]
        outer[half]["low_up"].wait_recv()
        up = send(queries.at[half, 3, pl.ds(0, 2)], queries.at[half, 2, pl.ds(0, 2)], at_axis(axis, 1))
        outer[half]["high_down"].wait_recv()
        down = send(queries.at[half, 1, pl.ds(2, 2)], queries.at[half, 2, pl.ds(2, 2)], at_axis(axis, 3))
        relay.append((up, down))

    parts = [[], []]

    def attend_and_send(half, step):
        attend(half, step, part_out.at[half, step])
        parts[half].append(
            send(part_out.at[half, step], part_in.at[half, SIDE - step], at_axis(axes[half][1], step))
        )

    for half in range(2):
        outer[half]["high_up"].wait_recv()
        attend_and_send(half, 3)
    for half in range(2):
        outer[half]["low_down"].wait_recv()
        attend_and_send(half, 1)
    for half in range(2):
        for copy in relay[half]:
            copy.wait_recv()
        attend_and_send(half, 2)

    for half in range(2):
        weight_finish(wr, half, outer_r[half], relay_r[half], shared_r)
    for copy in shared_r:
        copy.wait_recv()
    for core in range(2):
        for half in range(2):
            first = (core * 2 + half) * QUARTER
            projected = jnp.dot(
                normed[...],
                wr[core, half, :, :, :, 0:QUARTER].reshape(D, QUARTER),
                preferred_element_type=F32,
            )
            active = silu(projected + bias_ref[:, first : first + QUARTER])
            gates[:, first : first + QUARTER] = active.astype(BF16)

    totals, sums = [], []
    for half in range(2):
        for copy in parts[half]:
            copy.wait_recv()
        summed = []
        for inner_step in range(SIDE):
            total = own[half, inner_step]
            for step in range(1, SIDE):
                total += part_in[half, step, inner_step].astype(F32)
            summed.append(total)
        copies = []
        for step in (2, 1, 3):
            sum_out[half, step] = summed[step].astype(BF16)
            copies.append(
                send(sum_out.at[half, step], sum_in.at[half, SIDE - step], at_axis(axes[half][0], step))
            )
        totals.append(summed[0])
        sums.append(copies)
    attended = []
    for half in range(2):
        for copy in sums[half]:
            copy.wait_recv()
        total = totals[half]
        for step in range(1, SIDE):
            total += sum_in[half, step].astype(F32)
        attended.append(total)

    gated = norm(jnp.concatenate(attended, axis=1), gain_mid_ref[...])
    gated = (gated * gates[...].astype(F32)).astype(BF16)
    live = hist * CAND + lax.broadcasted_iota(jnp.int32, (CAND, QUARTER), 0) < counts_ref[0]
    for core in range(2):
        for half in range(2):
            first = (core * 2 + half) * QUARTER
            mixed = jnp.dot(
                gated,
                wr[core, half, :, :, :, QUARTER : 2 * QUARTER].reshape(D, QUARTER),
                preferred_element_type=F32,
            )
            mixed += fetched[:, first : first + QUARTER].astype(F32)
            out_ref[:, first : first + QUARTER] = jnp.where(live, mixed, 0.0).astype(BF16)

    for copy in started:
        copy.wait_send()


def local(
    item_table,
    cand_owner,
    cand_row,
    counts,
    hist_keys,
    hist_values,
    gain_in,
    w_in,
    bias_in,
    gain_mid,
    w_out,
):
    vmem = pl.BlockSpec(memory_space=pltpu.VMEM)
    anywhere = pl.BlockSpec(memory_space=pl.ANY)
    events = hist_keys.shape[1]
    result = pl.pallas_call(
        kernel,
        out_shape=jax.ShapeDtypeStruct((CAND, D), BF16),
        in_specs=[
            anywhere,
            vmem,
            vmem,
            pl.BlockSpec(memory_space=pltpu.SMEM),
            anywhere,
            anywhere,
            vmem,
            anywhere,
            vmem,
            vmem,
            anywhere,
        ],
        out_specs=vmem,
        scratch_shapes=[
            pltpu.VMEM((2, ROWS, D), BF16),
            pltpu.VMEM((events, D), BF16),
            pltpu.VMEM((events, D), BF16),
            pltpu.VMEM((2, 2, SIDE, SIDE, SHARD, QUARTER), BF16),
            pltpu.VMEM((2, 2, SIDE, SIDE, SHARD, 2 * QUARTER), BF16),
            pltpu.VMEM((PLANES, 1, 128), jnp.int32),
            pltpu.VMEM((PLANES, 1, 128), jnp.int32),
            pltpu.VMEM((len(GROUPS), 256, 128), BF16),
            pltpu.VMEM((PLANES, MESSAGE, 128), BF16),
            pltpu.VMEM((CAND, D), BF16),
            pltpu.VMEM((CAND, D), BF16),
            pltpu.VMEM((CAND, D), BF16),
            pltpu.VMEM((2, SIDE, SIDE, CAND, HALF), BF16),
            pltpu.VMEM((2, SIDE, CAND, HALF), F32),
            pltpu.VMEM((2, SIDE, SIDE, CAND, HALF), BF16),
            pltpu.VMEM((2, SIDE, SIDE, CAND, HALF), BF16),
            pltpu.VMEM((2, SIDE, CAND, HALF), BF16),
            pltpu.VMEM((2, SIDE, CAND, HALF), BF16),
            pltpu.SemaphoreType.DMA((MESSAGES,)),
            pltpu.SemaphoreType.DMA((MESSAGES,)),
            pltpu.SemaphoreType.DMA((16,)),
        ],
        compiler_params=pltpu.CompilerParams(
            collective_id=0, has_side_effects=True, vmem_limit_bytes=63 << 20
        ),
        name="layer",
    )(
        item_table,
        cand_owner.reshape(1, CAND),
        cand_row,
        counts,
        hist_keys[0],
        hist_values[0],
        gain_in.reshape(1, D),
        w_in,
        bias_in.reshape(1, 2 * D),
        gain_mid.reshape(1, D),
        w_out,
    )
    return result[None]


def solution(mesh):
    placed = (
        P("users", None),
        P("users", "hist", None),
        P("users", "hist"),
        P("users"),
        P("users", "hist", None),
        P("users", "hist", None),
        P(),
        P("hist", None),
        P(),
        P(),
        P("hist", None),
    )
    return jax.shard_map(
        local, mesh=mesh, in_specs=placed, out_specs=P("users", "hist", None), check_vma=False
    )
```

```python
import functools

import jax
import jax.numpy as jnp
from jax import lax
from jax.experimental import pallas as pl
from jax.experimental.pallas import tpu as pltpu
from jax.sharding import PartitionSpec as P

MESH = pl.DeviceIdType.MESH
F32, BF16 = jnp.float32, jnp.bfloat16

HEADS = 8
HEAD = 128
D = 1024
HALF = D // 2
QUARTER = D // 4
CAND = 48
ROWS = 256
PLANES = 16
SIDE = 4
SHARD = D // (SIDE * SIDE)
SLOTS = 6
PIECES = 8
MESSAGE = SLOTS * PIECES
EPS = 1e-05
RELAYED = ((0, 1), (1, 1), (2, 3), (3, 3))
SEMAPHORES = 81

GROUPS = ((1, 15, 2, 14), (3, 13, 4, 12), (5, 11, 6, 10), (7, 9, 8, 0))


def norm(values, gain):
    mean = jnp.mean(values, axis=-1, keepdims=True)
    centred = values - mean
    spread = jnp.mean(centred * centred, axis=-1, keepdims=True)
    return centred * lax.rsqrt(spread + EPS) * gain


def silu(values, scale=1.0):
    half = values * (0.5 * scale)
    return half + half * jnp.tanh(half)


def kernel(
    table_hbm,
    owner_hbm,
    row_hbm,
    counts_hbm,
    keys_hbm,
    values_hbm,
    gain_in_hbm,
    w_in_ref,
    bias_hbm,
    gain_mid_hbm,
    w_out_ref,
    out_ref,
    owner_row_ref,
    row_row_ref,
    counts_ref,
    gain_in_ref,
    bias_ref,
    gain_mid_ref,
    table,
    keys,
    values,
    wq,
    wr,
    plan,
    asked,
    spread,
    served,
    rows,
    fetched,
    normed,
    gates,
    queries,
    own,
    part_out,
    part_in,
    sum_out,
    sum_in,
    semaphores,
):
    users, hist = lax.axis_index("users"), lax.axis_index("hist")
    z, c = users // 2, lax.rem(users, 2)
    x, y = hist // SIDE, lax.rem(hist, SIDE)

    def at_z(step):
        return (lax.rem(z + step, PLANES) * 2 + c, hist)

    def at_axis(axis, step):
        if axis == "x":
            return (users, lax.rem(x + step, SIDE) * SIDE + y)
        return (users, x * SIDE + lax.rem(y + step, SIDE))

    partner = (z * 2 + 1 - c, hist)
    used, unsent = [], []

    def new():
        used.append(0)
        return semaphores.at[len(used) - 1]

    def send(src, dst, device, sent, landed):
        pltpu.make_async_remote_copy(
            src_ref=src,
            dst_ref=dst,
            send_sem=sent,
            recv_sem=landed,
            device_id=device,
            device_id_type=MESH,
        ).start()

    def wait(semaphore, like):
        pltpu.make_async_copy(like, like, semaphore).wait()

    def sending(like):
        semaphore = new()
        unsent.append((semaphore, like))
        return semaphore

    barrier = pltpu.get_barrier_semaphore()
    peers = [at_z(step) for step in range(1, PLANES)] + [partner]
    peers += [at_axis(axis, step) for axis in "xy" for step in range(1, SIDE)]
    for peer in peers:
        pl.semaphore_signal(barrier, inc=1, device_id=peer, device_id_type=MESH)

    def load(src, dst):
        copy = pltpu.make_async_copy(src, dst, new())
        copy.start()
        return copy

    load_small = [load(owner_hbm, owner_row_ref), load(row_hbm, row_row_ref)]
    load_weights = new()
    for core in range(2):
        for half in range(2):
            first = (core * 2 + half) * QUARTER
            mine = wr.at[core, half, x, y]
            for src, dst in (
                (w_in_ref.at[:, pl.ds(D + first, QUARTER)], wq.at[core, half, x, y]),
                (w_in_ref.at[:, pl.ds(first, QUARTER)], mine.at[:, pl.ds(0, QUARTER)]),
                (w_out_ref.at[:, pl.ds(first, QUARTER)], mine.at[:, pl.ds(QUARTER, QUARTER)]),
            ):
                pltpu.make_async_copy(src, dst, load_weights).start()
    load_table = load(table_hbm, table.at[c])
    load_late = [
        load(gain_in_hbm, gain_in_ref),
        load(bias_hbm, bias_ref),
        load(gain_mid_hbm, gain_mid_ref),
        load(counts_hbm, counts_ref),
        load(keys_hbm, keys),
        load(values_hbm, values),
    ]

    for copy in load_small:
        copy.wait()

    chip_row = ((owner_row_ref[...] >> 1) - z) & (PLANES - 1)
    later = lax.broadcasted_iota(jnp.int32, (CAND, CAND), 0)
    earlier = lax.broadcasted_iota(jnp.int32, (CAND, CAND), 1)
    chip_col = jnp.where(earlier == later, chip_row.astype(F32), 0.0)
    chip_col = jnp.sum(chip_col, axis=1, keepdims=True).astype(jnp.int32)
    before = earlier < later
    same = jnp.where((chip_col == chip_row) & before, 1.0, 0.0)
    rank = jnp.sum(same, axis=1, keepdims=True).astype(jnp.int32)
    lane = lax.broadcasted_iota(jnp.int32, (CAND, 128), 1) & 7
    slot_of = jnp.where(lane == rank, 1.0, 0.0).astype(BF16)
    chip_of = chip_row == lax.broadcasted_iota(jnp.int32, (PLANES, CAND), 0)
    row_part = jnp.where(chip_of, row_row_ref[...].astype(F32), 0.0).astype(BF16)
    core_part = jnp.where(chip_of, ((owner_row_ref[...] & 1) + 1).astype(F32), 0.0).astype(BF16)
    wanted = jnp.dot(row_part, slot_of, preferred_element_type=F32)
    wanted += (jnp.dot(core_part, slot_of, preferred_element_type=F32) - 1.0) * ROWS
    wanted = wanted.astype(jnp.int32)
    for step in range(PLANES):
        plan[step] = wanted[step : step + 1]
    asked[0] = wanted[0:1]

    wait(load_weights, wq.at[0, 0, pl.ds(0, 3)])
    pl.semaphore_wait(barrier, len(peers))

    table_landed = new()
    send(table_hbm, table.at[c], partner, sending(table_hbm), table_landed)
    ask_sent = sending(plan.at[pl.ds(1, PLANES - 1)])
    ask_landed = [new() for _ in GROUPS]
    for step in (8, 7, 9, 6, 10, 5, 11, 4, 12, 3, 13, 2, 14, 1, 15):
        (index,) = [i for i, steps in enumerate(GROUPS) if PLANES - step in steps]
        send(plan.at[step], asked.at[PLANES - step], at_z(step), ask_sent, ask_landed[index])

    axes = (("y", "x"), ("x", "y"))

    def block(buffer, half, outer, inner):
        if half == 0:
            return buffer.at[c, 0, lax.rem(x + outer, SIDE), lax.rem(y + inner, SIDE)]
        return buffer.at[c, 1, lax.rem(x + inner, SIDE), lax.rem(y + outer, SIDE)]

    def group(buffer, half, outer, first, count):
        if half == 0:
            return buffer.at[c, 0, lax.rem(x + outer, SIDE), pl.ds(first, count)]
        return buffer.at[c, 1, pl.ds(first, count), lax.rem(y + outer, SIDE)]

    def several(buffer, outer):
        return buffer.at[0, :, pl.ds(0, 3)] if outer else buffer.at[0, :, 0, pl.ds(0, 3)]

    class Gather:
        def __init__(self, buffer):
            self.buffer = buffer
            self.two, self.four = buffer.at[0, 0, 0, pl.ds(0, 2)], buffer.at[0, 0, 0]
            self.inner_sent, self.outer_sent = sending(several(buffer, 0)), sending(several(buffer, 1))
            self.share_sent = [sending(several(buffer, 0)), sending(several(buffer, 1))]
            self.share_landed = [new(), new()]
            self.inner_landed = new()
            self.landed = [[new() for _ in range(5)] for _ in range(2)]

        def inner(self):
            for half in range(2):
                mine = block(self.buffer, half, 0, 0)
                for step in (2, 1, 3):
                    send(mine, mine, at_axis(axes[half][0], step), self.inner_sent, self.inner_landed)

        def outer(self):
            wait(self.inner_landed, several(self.buffer, 0))
            for half in range(2):
                for index, (first, step) in enumerate(((0, 1), (2, 3), (2, 1), (0, 3))):
                    part = group(self.buffer, half, 0, first, 2)
                    device = at_axis(axes[half][1], step)
                    send(part, part, device, self.outer_sent, self.landed[half][index])

        def share_inner(self):
            for half in range(2):
                for step in range(1, SIDE):
                    part = block(self.buffer, half, 0, step)
                    send(part, part, partner, self.share_sent[0], self.share_landed[0])

        def relay(self):
            for half in range(2):
                for index, (first, step) in enumerate(((0, 1), (2, 3))):
                    wait(self.landed[half][index], self.two)
                    part = group(self.buffer, half, SIDE - step, first, 2)
                    device = at_axis(axes[half][1], step)
                    send(part, part, device, self.outer_sent, self.landed[half][4])

        def finish(self):
            for half in range(2):
                for index, outer, like in ((2, 3, self.two), (3, 1, self.two), (4, 2, self.four)):
                    wait(self.landed[half][index], like)
                    part = group(self.buffer, half, outer, 0, SIDE)
                    send(part, part, partner, self.share_sent[1], self.share_landed[1])

        def ready(self):
            wait(self.share_landed[0], several(self.buffer, 0))
            wait(self.share_landed[1], several(self.buffer, 1))

    gather_q, gather_r = Gather(wq), Gather(wr)
    gather_q.inner()

    load_table.wait()
    wait(table_landed, table.at[0])
    lanes = lax.broadcasted_iota(jnp.int32, (1, 128), 1)
    items = lax.broadcasted_iota(jnp.int32, (2 * ROWS, 128), 0)
    answer_sent, answer_landed = sending(rows.at[pl.ds(1, PLANES - 1)]), new()

    def serve(index):
        steps = GROUPS[index]
        wait(ask_landed[index], asked.at[pl.ds(1, len([step for step in steps if step]))])
        want = asked[steps[0]]
        for place in range(1, SIDE):
            want = jnp.where(lanes >> 3 == place, asked[steps[place]], want)
        picks = jnp.where((items == want) & (lanes < 32), 1.0, 0.0).astype(BF16)
        found = lax.dot_general(
            picks, table[...].reshape(2 * ROWS, D), (((0,), (0,)), ((), ())), preferred_element_type=F32
        )
        for j in range(PIECES):
            spread[pl.ds(j, 32, stride=PIECES), :] = found[:32, j * 128 : (j + 1) * 128]
        served[index] = spread[...].astype(BF16)
        for place, step in enumerate(steps):
            if step:
                send(
                    served.at[index, pl.ds(place * 64, MESSAGE)],
                    rows.at[PLANES - step],
                    at_z(step),
                    answer_sent,
                    answer_landed,
                )
            else:
                rows[0] = served[index, place * 64 : place * 64 + MESSAGE]

    for index in range(len(GROUPS)):
        serve(index)
    gather_q.outer()
    gather_r.inner()
    gather_q.share_inner()
    gather_q.relay()
    gather_r.outer()
    gather_q.finish()
    gather_r.share_inner()

    wait(answer_landed, rows.at[pl.ds(1, PLANES - 1)])
    place = chip_col * MESSAGE + rank * PIECES
    column = lax.broadcasted_iota(jnp.int32, (CAND, PLANES * MESSAGE), 1)
    picks = jnp.concatenate(
        [jnp.where(column == place + j, 1.0, 0.0).astype(BF16) for j in range(PIECES)], axis=0
    )
    found = jnp.dot(picks, rows[...].reshape(PLANES * MESSAGE, 128), preferred_element_type=F32)
    for j in range(PIECES):
        fetched[:, j * 128 : (j + 1) * 128] = found[j * CAND : (j + 1) * CAND].astype(BF16)
    for copy in load_late:
        copy.wait()
    normed[...] = norm(fetched[...].astype(F32), gain_in_ref[...]).astype(BF16)

    gather_r.relay()
    gather_q.ready()
    for core in range(2):
        for half in range(2):
            first = (core * 2 + half) * QUARTER
            projected = jnp.dot(
                normed[...], wq[core, half].reshape(D, QUARTER), preferred_element_type=F32
            )
            active = silu(projected + bias_ref[:, D + first : D + first + QUARTER])
            queries[core, 0, 0, :, half * QUARTER : (half + 1) * QUARTER] = active.astype(BF16)

    query_sent = [sending(queries.at[:, 0, pl.ds(0, 3)]), sending(queries.at[:, pl.ds(0, 3)])]
    inner_landed = [{step: new() for step in (2, 1, 3)} for _ in range(2)]
    for half in range(2):
        mine = queries.at[half, 0, 0]
        for step in (2, 1, 3):
            send(
                mine,
                queries.at[half, 0, SIDE - step],
                at_axis(axes[half][0], step),
                query_sent[0],
                inner_landed[half][step],
            )
    outer_landed = []
    for half in range(2):
        landed = {step: new() for step in (1, 2, 3)}
        outer_landed.append((landed, {key: new() for key in RELAYED}))

    def send_block(half, place):
        for step in (1, 3):
            together, alone = outer_landed[half]
            send(
                queries.at[half, 0, place],
                queries.at[half, SIDE - step, place],
                at_axis(axes[half][1], step),
                query_sent[1],
                alone[place, step] if (place, step) in RELAYED else together[step],
            )

    def relay_block(half, place, step):
        together, alone = outer_landed[half]
        wait(alone[place, step], queries.at[half, 0, 0])
        send(
            queries.at[half, SIDE - step, place],
            queries.at[half, 2, place],
            at_axis(axes[half][1], step),
            query_sent[1],
            together[2],
        )

    for half in range(2):
        send_block(half, 0)
    for step, place in ((1, 3), (3, 1), (2, 2)):
        for half in range(2):
            wait(inner_landed[half][step], queries.at[half, 0, 0])
            send_block(half, place)

    def attend(half, step, target):
        scores = []
        for head in range(HEADS // 2):
            there = slice(head * HEAD, (head + 1) * HEAD)
            first = half * HALF + head * HEAD
            query = queries[half, step, :, :, there].reshape(SIDE * CAND, HEAD)
            scores.append(
                lax.dot_general(
                    query,
                    keys[:, first : first + HEAD],
                    (((1,), (1,)), ((), ())),
                    preferred_element_type=F32,
                )
            )
        for head in range(HEADS // 2):
            there = slice(head * HEAD, (head + 1) * HEAD)
            first = half * HALF + head * HEAD
            weights = silu(scores[head], HEAD**-0.5).astype(BF16)
            total = jnp.dot(weights, values[:, first : first + HEAD], preferred_element_type=F32)
            target[:, :, there] = total.reshape(SIDE, CAND, HEAD).astype(target.dtype)

    for half in range(2):
        attend(half, 0, own.at[half])

    for place, step in ((0, 1), (3, 3), (1, 1), (2, 3)):
        for half in range(2):
            relay_block(half, place, step)

    part_sent = sending(part_out.at[:, pl.ds(1, 3)])
    part_landed = [new() for _ in range(2)]

    def attend_and_send(half, step):
        attend(half, step, part_out.at[half, step])
        send(
            part_out.at[half, step],
            part_in.at[half, SIDE - step],
            at_axis(axes[half][1], step),
            part_sent,
            part_landed[half],
        )

    for step in (3, 1, 2):
        for half in range(2):
            count = 4 if step == 2 else 2
            wait(outer_landed[half][0][SIDE - step], queries.at[half, 0, pl.ds(0, count)])
            attend_and_send(half, step)

    gather_r.finish()
    gather_r.ready()
    for core in range(2):
        for half in range(2):
            first = (core * 2 + half) * QUARTER
            projected = jnp.dot(
                normed[...],
                wr[core, half, :, :, :, 0:QUARTER].reshape(D, QUARTER),
                preferred_element_type=F32,
            )
            active = silu(projected + bias_ref[:, first : first + QUARTER])
            gates[:, first : first + QUARTER] = active.astype(BF16)

    totals = []
    sum_sent = sending(sum_out.at[:, pl.ds(1, 3)])
    sum_landed = [new() for _ in range(2)]
    for half in range(2):
        wait(part_landed[half], part_in.at[half, pl.ds(1, 3)])
        summed = []
        for inner_step in range(SIDE):
            total = own[half, inner_step]
            for step in range(1, SIDE):
                total += part_in[half, step, inner_step].astype(F32)
            summed.append(total)
        for step in (2, 1, 3):
            sum_out[half, step] = summed[step].astype(BF16)
            send(
                sum_out.at[half, step],
                sum_in.at[half, SIDE - step],
                at_axis(axes[half][0], step),
                sum_sent,
                sum_landed[half],
            )
        totals.append(summed[0])
    attended = []
    for half in range(2):
        wait(sum_landed[half], sum_in.at[half, pl.ds(1, 3)])
        total = totals[half]
        for step in range(1, SIDE):
            total += sum_in[half, step].astype(F32)
        attended.append(total)

    gated = norm(jnp.concatenate(attended, axis=1), gain_mid_ref[...])
    gated = (gated * gates[...].astype(F32)).astype(BF16)
    live = hist * CAND + lax.broadcasted_iota(jnp.int32, (CAND, QUARTER), 0) < counts_ref[...]
    for core in range(2):
        for half in range(2):
            first = (core * 2 + half) * QUARTER
            mixed = jnp.dot(
                gated,
                wr[core, half, :, :, :, QUARTER : 2 * QUARTER].reshape(D, QUARTER),
                preferred_element_type=F32,
            )
            mixed += fetched[:, first : first + QUARTER].astype(F32)
            out_ref[:, first : first + QUARTER] = jnp.where(live, mixed, 0.0).astype(BF16)

    for semaphore, like in unsent:
        wait(semaphore, like)
    assert len(used) == SEMAPHORES, len(used)


def local(
    item_table,
    cand_owner,
    cand_row,
    counts,
    hist_keys,
    hist_values,
    gain_in,
    w_in,
    bias_in,
    gain_mid,
    w_out,
):
    vmem = pl.BlockSpec(memory_space=pltpu.VMEM)
    anywhere = pl.BlockSpec(memory_space=pl.ANY)
    events = hist_keys.shape[1]
    result = pl.pallas_call(
        kernel,
        out_shape=jax.ShapeDtypeStruct((CAND, D), BF16),
        in_specs=[anywhere] * 11,
        out_specs=vmem,
        scratch_shapes=[
            pltpu.VMEM((1, CAND), jnp.int32),
            pltpu.VMEM((1, CAND), jnp.int32),
            pltpu.VMEM((1, 1), jnp.int32),
            pltpu.VMEM((1, D), F32),
            pltpu.VMEM((1, 2 * D), F32),
            pltpu.VMEM((1, D), F32),
            pltpu.VMEM((2, ROWS, D), BF16),
            pltpu.VMEM((events, D), BF16),
            pltpu.VMEM((events, D), BF16),
            pltpu.VMEM((2, 2, SIDE, SIDE, SHARD, QUARTER), BF16),
            pltpu.VMEM((2, 2, SIDE, SIDE, SHARD, 2 * QUARTER), BF16),
            pltpu.VMEM((PLANES, 1, 128), jnp.int32),
            pltpu.VMEM((PLANES, 1, 128), jnp.int32),
            pltpu.VMEM((256, 128), F32),
            pltpu.VMEM((len(GROUPS), 256, 128), BF16),
            pltpu.VMEM((PLANES, MESSAGE, 128), BF16),
            pltpu.VMEM((CAND, D), BF16),
            pltpu.VMEM((CAND, D), BF16),
            pltpu.VMEM((CAND, D), BF16),
            pltpu.VMEM((2, SIDE, SIDE, CAND, HALF), BF16),
            pltpu.VMEM((2, SIDE, CAND, HALF), F32),
            pltpu.VMEM((2, SIDE, SIDE, CAND, HALF), BF16),
            pltpu.VMEM((2, SIDE, SIDE, CAND, HALF), BF16),
            pltpu.VMEM((2, SIDE, CAND, HALF), BF16),
            pltpu.VMEM((2, SIDE, CAND, HALF), BF16),
            pltpu.SemaphoreType.DMA((SEMAPHORES,)),
        ],
        compiler_params=pltpu.CompilerParams(
            collective_id=0, has_side_effects=True, vmem_limit_bytes=63 << 20
        ),
        name="layer",
    )(
        item_table,
        cand_owner.reshape(1, CAND),
        cand_row,
        counts.reshape(1, 1),
        hist_keys[0],
        hist_values[0],
        gain_in.reshape(1, D),
        w_in,
        bias_in.reshape(1, 2 * D),
        gain_mid.reshape(1, D),
        w_out,
    )
    return result[None]


def solution(mesh):
    placed = (
        P("users", None),
        P("users", "hist", None),
        P("users", "hist"),
        P("users"),
        P("users", "hist", None),
        P("users", "hist", None),
        P(),
        P("hist", None),
        P(),
        P(),
        P("hist", None),
    )
    return jax.shard_map(
        local, mesh=mesh, in_specs=placed, out_specs=P("users", "hist", None), check_vma=False
    )
```

```python
import functools

import jax
import jax.numpy as jnp
from jax import lax
from jax.experimental import pallas as pl
from jax.experimental.pallas import tpu as pltpu
from jax.sharding import PartitionSpec as P

MESH = pl.DeviceIdType.MESH
F32, BF16 = jnp.float32, jnp.bfloat16

HEADS = 8
HEAD = 128
D = 1024
HALF = D // 2
QUARTER = D // 4
CAND = 48
ROWS = 256
PLANES = 16
SIDE = 4
SHARD = D // (SIDE * SIDE)
SLOTS = 6
PIECES = 8
MESSAGE = SLOTS * PIECES
EPS = 1e-05
RELAYED = ((0, 1), (1, 1), (3, 3))
SEMAPHORES = 81

GROUPS = ((1, 15, 2, 14), (3, 13, 4, 12), (5, 11, 6, 10), (7, 9, 8, 0))


def norm(values, gain):
    mean = jnp.mean(values, axis=-1, keepdims=True)
    centred = values - mean
    spread = jnp.mean(centred * centred, axis=-1, keepdims=True)
    return centred * lax.rsqrt(spread + EPS) * gain


def silu(values, scale=1.0):
    half = values * (0.5 * scale)
    return half + half * jnp.tanh(half)


def kernel(
    table_hbm,
    owner_hbm,
    row_hbm,
    counts_hbm,
    keys_hbm,
    values_hbm,
    gain_in_hbm,
    w_in_ref,
    bias_hbm,
    gain_mid_hbm,
    w_out_ref,
    out_ref,
    owner_row_ref,
    row_row_ref,
    counts_ref,
    gain_in_ref,
    bias_ref,
    gain_mid_ref,
    table,
    keys,
    values,
    wq,
    wr,
    plan,
    asked,
    spread,
    served,
    rows,
    fetched,
    normed,
    gates,
    queries,
    own,
    part_out,
    part_in,
    sum_out,
    sum_in,
    semaphores,
):
    users, hist = lax.axis_index("users"), lax.axis_index("hist")
    z, c = users // 2, lax.rem(users, 2)
    x, y = hist // SIDE, lax.rem(hist, SIDE)

    def at_z(step):
        return (lax.rem(z + step, PLANES) * 2 + c, hist)

    def at_axis(axis, step):
        if axis == "x":
            return (users, lax.rem(x + step, SIDE) * SIDE + y)
        return (users, x * SIDE + lax.rem(y + step, SIDE))

    partner = (z * 2 + 1 - c, hist)
    used, unsent = [], []

    def new():
        used.append(0)
        return semaphores.at[len(used) - 1]

    def send(src, dst, device, sent, landed):
        pltpu.make_async_remote_copy(
            src_ref=src,
            dst_ref=dst,
            send_sem=sent,
            recv_sem=landed,
            device_id=device,
            device_id_type=MESH,
        ).start()

    def wait(semaphore, like):
        pltpu.make_async_copy(like, like, semaphore).wait()

    def sending(like):
        semaphore = new()
        unsent.append((semaphore, like))
        return semaphore

    barrier = pltpu.get_barrier_semaphore()
    peers = [at_z(step) for step in range(1, PLANES)] + [partner]
    peers += [at_axis(axis, step) for axis in "xy" for step in range(1, SIDE)]
    for peer in peers:
        pl.semaphore_signal(barrier, inc=1, device_id=peer, device_id_type=MESH)

    def load(src, dst):
        copy = pltpu.make_async_copy(src, dst, new())
        copy.start()
        return copy

    load_small = [load(owner_hbm, owner_row_ref), load(row_hbm, row_row_ref)]
    load_weights = new()
    for core in range(2):
        for half in range(2):
            first = (core * 2 + half) * QUARTER
            mine = wr.at[core, half, x, y]
            for src, dst in (
                (w_in_ref.at[:, pl.ds(D + first, QUARTER)], wq.at[core, half, x, y]),
                (w_in_ref.at[:, pl.ds(first, QUARTER)], mine.at[:, pl.ds(0, QUARTER)]),
                (w_out_ref.at[:, pl.ds(first, QUARTER)], mine.at[:, pl.ds(QUARTER, QUARTER)]),
            ):
                pltpu.make_async_copy(src, dst, load_weights).start()
    load_table = load(table_hbm, table.at[c])
    load_late = [
        load(gain_in_hbm, gain_in_ref),
        load(bias_hbm, bias_ref),
        load(gain_mid_hbm, gain_mid_ref),
        load(counts_hbm, counts_ref),
        load(keys_hbm, keys),
        load(values_hbm, values),
    ]

    for copy in load_small:
        copy.wait()

    chip_row = ((owner_row_ref[...] >> 1) - z) & (PLANES - 1)
    later = lax.broadcasted_iota(jnp.int32, (CAND, CAND), 0)
    earlier = lax.broadcasted_iota(jnp.int32, (CAND, CAND), 1)
    chip_col = jnp.where(earlier == later, chip_row.astype(F32), 0.0)
    chip_col = jnp.sum(chip_col, axis=1, keepdims=True).astype(jnp.int32)
    before = earlier < later
    same = jnp.where((chip_col == chip_row) & before, 1.0, 0.0)
    rank = jnp.sum(same, axis=1, keepdims=True).astype(jnp.int32)
    lane = lax.broadcasted_iota(jnp.int32, (CAND, 128), 1) & 7
    slot_of = jnp.where(lane == rank, 1.0, 0.0).astype(BF16)
    chip_of = chip_row == lax.broadcasted_iota(jnp.int32, (PLANES, CAND), 0)
    row_part = jnp.where(chip_of, row_row_ref[...].astype(F32), 0.0).astype(BF16)
    core_part = jnp.where(chip_of, ((owner_row_ref[...] & 1) + 1).astype(F32), 0.0).astype(BF16)
    wanted = jnp.dot(row_part, slot_of, preferred_element_type=F32)
    wanted += (jnp.dot(core_part, slot_of, preferred_element_type=F32) - 1.0) * ROWS
    wanted = wanted.astype(jnp.int32)
    for step in range(PLANES):
        plan[step] = wanted[step : step + 1]
    asked[0] = wanted[0:1]

    wait(load_weights, wq.at[0, 0, pl.ds(0, 3)])
    pl.semaphore_wait(barrier, len(peers))

    table_landed = new()
    send(table_hbm, table.at[c], partner, sending(table_hbm), table_landed)
    ask_sent = sending(plan.at[pl.ds(1, PLANES - 1)])
    ask_landed = [new() for _ in GROUPS]
    for step in (8, 7, 9, 6, 10, 5, 11, 4, 12, 3, 13, 2, 14, 1, 15):
        (index,) = [i for i, steps in enumerate(GROUPS) if PLANES - step in steps]
        send(plan.at[step], asked.at[PLANES - step], at_z(step), ask_sent, ask_landed[index])

    axes = (("y", "x"), ("x", "y"))

    def block(buffer, half, outer, inner):
        if half == 0:
            return buffer.at[c, 0, lax.rem(x + outer, SIDE), lax.rem(y + inner, SIDE)]
        return buffer.at[c, 1, lax.rem(x + inner, SIDE), lax.rem(y + outer, SIDE)]

    def group(buffer, half, outer, first, count):
        if half == 0:
            return buffer.at[c, 0, lax.rem(x + outer, SIDE), pl.ds(first, count)]
        return buffer.at[c, 1, pl.ds(first, count), lax.rem(y + outer, SIDE)]

    def several(buffer, outer):
        return buffer.at[0, :, pl.ds(0, 3)] if outer else buffer.at[0, :, 0, pl.ds(0, 3)]

    class Gather:
        def __init__(self, buffer):
            self.buffer = buffer
            self.two, self.four = buffer.at[0, 0, 0, pl.ds(0, 2)], buffer.at[0, 0, 0]
            self.inner_sent, self.outer_sent = sending(several(buffer, 0)), sending(several(buffer, 1))
            self.share_sent = [sending(several(buffer, 0)), sending(several(buffer, 1))]
            self.share_landed = [new(), new()]
            self.inner_landed = new()
            self.landed = [[new() for _ in range(5)] for _ in range(2)]

        def inner(self):
            for half in range(2):
                mine = block(self.buffer, half, 0, 0)
                for step in (2, 1, 3):
                    send(mine, mine, at_axis(axes[half][0], step), self.inner_sent, self.inner_landed)

        def outer(self):
            wait(self.inner_landed, several(self.buffer, 0))
            for half in range(2):
                for index, (first, step) in enumerate(((0, 1), (2, 3), (2, 1), (0, 3))):
                    part = group(self.buffer, half, 0, first, 2)
                    device = at_axis(axes[half][1], step)
                    send(part, part, device, self.outer_sent, self.landed[half][index])

        def share_inner(self):
            for half in range(2):
                for step in range(1, SIDE):
                    part = block(self.buffer, half, 0, step)
                    send(part, part, partner, self.share_sent[0], self.share_landed[0])

        def relay(self):
            for half in range(2):
                for index, (first, step) in enumerate(((0, 1), (2, 3))):
                    wait(self.landed[half][index], self.two)
                    part = group(self.buffer, half, SIDE - step, first, 2)
                    device = at_axis(axes[half][1], step)
                    send(part, part, device, self.outer_sent, self.landed[half][4])

        def finish(self):
            for half in range(2):
                for index, outer, like in ((2, 3, self.two), (3, 1, self.two), (4, 2, self.four)):
                    wait(self.landed[half][index], like)
                    part = group(self.buffer, half, outer, 0, SIDE)
                    send(part, part, partner, self.share_sent[1], self.share_landed[1])

        def ready(self):
            wait(self.share_landed[0], several(self.buffer, 0))
            wait(self.share_landed[1], several(self.buffer, 1))

    gather_q, gather_r = Gather(wq), Gather(wr)
    gather_q.inner()

    load_table.wait()
    wait(table_landed, table.at[0])
    lanes = lax.broadcasted_iota(jnp.int32, (1, 128), 1)
    items = lax.broadcasted_iota(jnp.int32, (2 * ROWS, 128), 0)
    answer_sent, answer_landed = sending(rows.at[pl.ds(1, PLANES - 1)]), new()

    def serve(index):
        steps = GROUPS[index]
        wait(ask_landed[index], asked.at[pl.ds(1, len([step for step in steps if step]))])
        want = asked[steps[0]]
        for place in range(1, SIDE):
            want = jnp.where(lanes >> 3 == place, asked[steps[place]], want)
        picks = jnp.where((items == want) & (lanes < 32), 1.0, 0.0).astype(BF16)
        found = lax.dot_general(
            picks, table[...].reshape(2 * ROWS, D), (((0,), (0,)), ((), ())), preferred_element_type=F32
        )
        for j in range(PIECES):
            spread[pl.ds(j, 32, stride=PIECES), :] = found[:32, j * 128 : (j + 1) * 128]
        served[index] = spread[...].astype(BF16)
        for place, step in enumerate(steps):
            if step:
                send(
                    served.at[index, pl.ds(place * 64, MESSAGE)],
                    rows.at[PLANES - step],
                    at_z(step),
                    answer_sent,
                    answer_landed,
                )
            else:
                rows[0] = served[index, place * 64 : place * 64 + MESSAGE]

    serve(0)
    serve(1)
    gather_q.outer()
    serve(2)
    serve(3)
    gather_r.inner()
    gather_q.share_inner()
    gather_q.relay()
    gather_r.outer()
    gather_q.finish()
    gather_r.share_inner()

    wait(answer_landed, rows.at[pl.ds(1, PLANES - 1)])
    place = chip_col * MESSAGE + rank * PIECES
    column = lax.broadcasted_iota(jnp.int32, (CAND, PLANES * MESSAGE), 1)
    picks = jnp.concatenate(
        [jnp.where(column == place + j, 1.0, 0.0).astype(BF16) for j in range(PIECES)], axis=0
    )
    found = jnp.dot(picks, rows[...].reshape(PLANES * MESSAGE, 128), preferred_element_type=F32)
    for j in range(PIECES):
        fetched[:, j * 128 : (j + 1) * 128] = found[j * CAND : (j + 1) * CAND].astype(BF16)
    for copy in load_late:
        copy.wait()
    normed[...] = norm(fetched[...].astype(F32), gain_in_ref[...]).astype(BF16)

    gather_r.relay()
    gather_q.ready()

    query_sent = [sending(queries.at[:, 0, pl.ds(0, 3)]), sending(queries.at[:, pl.ds(0, 3)])]
    inner_landed = [{step: new() for step in (2, 1, 3)} for _ in range(2)]
    outer_landed = []
    for half in range(2):
        landed = {key: new() for key in (1, 3, "low", "high")}
        outer_landed.append((landed, {key: new() for key in RELAYED}))

    def send_block(half, place):
        together, alone = outer_landed[half]
        for step in (2, 1, 3) if place == 2 else (1, 3):
            landed = together["high" if step == 2 else step]
            send(
                queries.at[half, 0, place],
                queries.at[half, SIDE - step, place],
                at_axis(axes[half][1], step),
                query_sent[1],
                alone[place, step] if (place, step) in RELAYED else landed,
            )

    def relay_block(half, place, step):
        together, alone = outer_landed[half]
        wait(alone[place, step], queries.at[half, 0, 0])
        send(
            queries.at[half, SIDE - step, place],
            queries.at[half, 2, place],
            at_axis(axes[half][1], step),
            query_sent[1],
            together["low" if place < 2 else "high"],
        )

    for half in range(2):
        for piece in range(2):
            first = D + half * HALF + piece * QUARTER
            projected = jnp.dot(
                normed[...], wq[half, piece].reshape(D, QUARTER), preferred_element_type=F32
            )
            active = silu(projected + bias_ref[:, first : first + QUARTER])
            queries[half, 0, 0, :, piece * QUARTER : (piece + 1) * QUARTER] = active.astype(BF16)
        for step in (2, 1, 3):
            send(
                queries.at[half, 0, 0],
                queries.at[half, 0, SIDE - step],
                at_axis(axes[half][0], step),
                query_sent[0],
                inner_landed[half][step],
            )
        send_block(half, 0)
    for step, place in ((1, 3), (3, 1), (2, 2)):
        for half in range(2):
            wait(inner_landed[half][step], queries.at[half, 0, 0])
            send_block(half, place)

    def attend(half, step, target, first_block=0, count=SIDE):
        blocks = slice(first_block, first_block + count)
        scores = []
        for head in range(HEADS // 2):
            there = slice(head * HEAD, (head + 1) * HEAD)
            first = half * HALF + head * HEAD
            query = queries[half, step, blocks, :, there].reshape(count * CAND, HEAD)
            scores.append(
                lax.dot_general(
                    query,
                    keys[:, first : first + HEAD],
                    (((1,), (1,)), ((), ())),
                    preferred_element_type=F32,
                )
            )
        for head in range(HEADS // 2):
            there = slice(head * HEAD, (head + 1) * HEAD)
            first = half * HALF + head * HEAD
            weights = silu(scores[head], HEAD**-0.5).astype(BF16)
            total = jnp.dot(weights, values[:, first : first + HEAD], preferred_element_type=F32)
            target[blocks, :, there] = total.reshape(count, CAND, HEAD).astype(target.dtype)

    for half in range(2):
        attend(half, 0, own.at[half])

    for place, step in ((0, 1), (3, 3), (1, 1)):
        for half in range(2):
            relay_block(half, place, step)

    part_sent = sending(part_out.at[:, pl.ds(1, 3)])
    part_landed = [new() for _ in range(2)]

    def attend_and_send(half, step, first, count):
        attend(half, step, part_out.at[half, step], first, count)
        blocks = pl.ds(first, count)
        send(
            part_out.at[half, step, blocks],
            part_in.at[half, SIDE - step, blocks],
            at_axis(axes[half][1], step),
            part_sent,
            part_landed[half],
        )

    for step, first, count, key, landed in (
        (3, 0, SIDE, 1, 2),
        (1, 0, SIDE, 3, 3),
        (2, 0, 2, "low", 2),
        (2, 2, 2, "high", 2),
    ):
        for half in range(2):
            wait(outer_landed[half][0][key], queries.at[half, 0, pl.ds(0, landed)])
            attend_and_send(half, step, first, count)

    gather_r.finish()
    gather_r.ready()
    for core in range(2):
        for half in range(2):
            first = (core * 2 + half) * QUARTER
            projected = jnp.dot(
                normed[...],
                wr[core, half, :, :, :, 0:QUARTER].reshape(D, QUARTER),
                preferred_element_type=F32,
            )
            active = silu(projected + bias_ref[:, first : first + QUARTER])
            gates[:, first : first + QUARTER] = active.astype(BF16)

    totals = []
    sum_sent = sending(sum_out.at[:, pl.ds(1, 3)])
    sum_landed = [new() for _ in range(2)]
    for half in range(2):
        wait(part_landed[half], part_in.at[half, pl.ds(1, 3)])

        def summed(place):
            total = own[half, place]
            for step in range(1, SIDE):
                total += part_in[half, step, place].astype(F32)
            return total

        for step in (2, 1, 3):
            sum_out[half, step] = summed(step).astype(BF16)
            send(
                sum_out.at[half, step],
                sum_in.at[half, SIDE - step],
                at_axis(axes[half][0], step),
                sum_sent,
                sum_landed[half],
            )
        totals.append(summed(0))
    attended = []
    for half in range(2):
        wait(sum_landed[half], sum_in.at[half, pl.ds(1, 3)])
        total = totals[half]
        for step in range(1, SIDE):
            total += sum_in[half, step].astype(F32)
        attended.append(total)

    gated = norm(jnp.concatenate(attended, axis=1), gain_mid_ref[...])
    gated = (gated * gates[...].astype(F32)).astype(BF16)
    live = hist * CAND + lax.broadcasted_iota(jnp.int32, (CAND, QUARTER), 0) < counts_ref[...]
    for core in range(2):
        for half in range(2):
            first = (core * 2 + half) * QUARTER
            mixed = jnp.dot(
                gated,
                wr[core, half, :, :, :, QUARTER : 2 * QUARTER].reshape(D, QUARTER),
                preferred_element_type=F32,
            )
            mixed += fetched[:, first : first + QUARTER].astype(F32)
            out_ref[:, first : first + QUARTER] = jnp.where(live, mixed, 0.0).astype(BF16)

    for semaphore, like in unsent:
        wait(semaphore, like)
    assert len(used) == SEMAPHORES, len(used)


def local(
    item_table,
    cand_owner,
    cand_row,
    counts,
    hist_keys,
    hist_values,
    gain_in,
    w_in,
    bias_in,
    gain_mid,
    w_out,
):
    vmem = pl.BlockSpec(memory_space=pltpu.VMEM)
    anywhere = pl.BlockSpec(memory_space=pl.ANY)
    events = hist_keys.shape[1]
    result = pl.pallas_call(
        kernel,
        out_shape=jax.ShapeDtypeStruct((CAND, D), BF16),
        in_specs=[anywhere] * 11,
        out_specs=vmem,
        scratch_shapes=[
            pltpu.VMEM((1, CAND), jnp.int32),
            pltpu.VMEM((1, CAND), jnp.int32),
            pltpu.VMEM((1, 1), jnp.int32),
            pltpu.VMEM((1, D), F32),
            pltpu.VMEM((1, 2 * D), F32),
            pltpu.VMEM((1, D), F32),
            pltpu.VMEM((2, ROWS, D), BF16),
            pltpu.VMEM((events, D), BF16),
            pltpu.VMEM((events, D), BF16),
            pltpu.VMEM((2, 2, SIDE, SIDE, SHARD, QUARTER), BF16),
            pltpu.VMEM((2, 2, SIDE, SIDE, SHARD, 2 * QUARTER), BF16),
            pltpu.VMEM((PLANES, 1, 128), jnp.int32),
            pltpu.VMEM((PLANES, 1, 128), jnp.int32),
            pltpu.VMEM((256, 128), F32),
            pltpu.VMEM((len(GROUPS), 256, 128), BF16),
            pltpu.VMEM((PLANES, MESSAGE, 128), BF16),
            pltpu.VMEM((CAND, D), BF16),
            pltpu.VMEM((CAND, D), BF16),
            pltpu.VMEM((CAND, D), BF16),
            pltpu.VMEM((2, SIDE, SIDE, CAND, HALF), BF16),
            pltpu.VMEM((2, SIDE, CAND, HALF), F32),
            pltpu.VMEM((2, SIDE, SIDE, CAND, HALF), BF16),
            pltpu.VMEM((2, SIDE, SIDE, CAND, HALF), BF16),
            pltpu.VMEM((2, SIDE, CAND, HALF), BF16),
            pltpu.VMEM((2, SIDE, CAND, HALF), BF16),
            pltpu.SemaphoreType.DMA((SEMAPHORES,)),
        ],
        compiler_params=pltpu.CompilerParams(
            collective_id=0, has_side_effects=True, vmem_limit_bytes=63 << 20
        ),
        name="layer",
    )(
        item_table,
        cand_owner.reshape(1, CAND),
        cand_row,
        counts.reshape(1, 1),
        hist_keys[0],
        hist_values[0],
        gain_in.reshape(1, D),
        w_in,
        bias_in.reshape(1, 2 * D),
        gain_mid.reshape(1, D),
        w_out,
    )
    return result[None]


def solution(mesh):
    placed = (
        P("users", None),
        P("users", "hist", None),
        P("users", "hist"),
        P("users"),
        P("users", "hist", None),
        P("users", "hist", None),
        P(),
        P("hist", None),
        P(),
        P(),
        P("hist", None),
    )
    return jax.shard_map(
        local, mesh=mesh, in_specs=placed, out_specs=P("users", "hist", None), check_vma=False
    )
```

```python
import functools

import jax
import jax.numpy as jnp
from jax import lax
from jax.experimental import pallas as pl
from jax.experimental.pallas import tpu as pltpu
from jax.sharding import PartitionSpec as P

MESH = pl.DeviceIdType.MESH
F32, BF16 = jnp.float32, jnp.bfloat16

HEADS = 8
HEAD = 128
D = 1024
HALF = D // 2
QUARTER = D // 4
CAND = 48
ROWS = 256
PLANES = 16
SIDE = 4
SHARD = D // (SIDE * SIDE)
SLOTS = 6
PIECES = 8
MESSAGE = SLOTS * PIECES
EPS = 1e-05
RELAYED = ((0, 1), (1, 1), (3, 3))
SEMAPHORES = 85

GROUPS = ((1, 15, 2, 14), (3, 13, 4, 12), (5, 11, 6, 10), (7, 9, 8, 0))


def norm(values, gain):
    mean = jnp.mean(values, axis=-1, keepdims=True)
    centred = values - mean
    spread = jnp.mean(centred * centred, axis=-1, keepdims=True)
    return centred * lax.rsqrt(spread + EPS) * gain


def silu(values, scale=1.0):
    half = values * (0.5 * scale)
    return half + half * jnp.tanh(half)


def kernel(
    table_hbm,
    owner_hbm,
    row_hbm,
    counts_hbm,
    keys_hbm,
    values_hbm,
    gain_in_hbm,
    w_in_ref,
    bias_hbm,
    gain_mid_hbm,
    w_out_ref,
    out_hbm,
    out_ref,
    owner_row_ref,
    row_row_ref,
    counts_ref,
    gain_in_ref,
    bias_ref,
    gain_mid_ref,
    table,
    keys,
    values,
    wq,
    wr,
    plan,
    asked,
    order,
    spread,
    served,
    rows,
    fetched,
    normed,
    gates,
    queries,
    own,
    part_out,
    part_in,
    sum_out,
    sum_in,
    semaphores,
):
    users, hist = lax.axis_index("users"), lax.axis_index("hist")
    z, c = users // 2, lax.rem(users, 2)
    x, y = hist // SIDE, lax.rem(hist, SIDE)

    def at_z(step):
        return (lax.rem(z + step, PLANES) * 2 + c, hist)

    def at_axis(axis, step):
        if axis == "x":
            return (users, lax.rem(x + step, SIDE) * SIDE + y)
        return (users, x * SIDE + lax.rem(y + step, SIDE))

    partner = (z * 2 + 1 - c, hist)
    used, unsent = [], []

    def new():
        used.append(0)
        return semaphores.at[len(used) - 1]

    def send(src, dst, device, sent, landed):
        pltpu.make_async_remote_copy(
            src_ref=src,
            dst_ref=dst,
            send_sem=sent,
            recv_sem=landed,
            device_id=device,
            device_id_type=MESH,
        ).start()

    def wait(semaphore, like):
        pltpu.make_async_copy(like, like, semaphore).wait()

    def sending(like):
        semaphore = new()
        unsent.append((semaphore, like))
        return semaphore

    barrier = pltpu.get_barrier_semaphore()
    far_first = (8, 7, 9, 6, 10, 5, 11, 4, 12, 3, 13, 2, 14, 1, 15)
    peers = [at_z(step) for step in far_first] + [partner]
    peers += [at_axis(axis, step) for axis in "xy" for step in range(1, SIDE)]
    for peer in peers:
        pl.semaphore_signal(barrier, inc=1, device_id=peer, device_id_type=MESH)

    def load(src, dst):
        copy = pltpu.make_async_copy(src, dst, new())
        copy.start()
        return copy

    load_small = [load(owner_hbm, owner_row_ref), load(row_hbm, row_row_ref)]
    load_weights = new()
    for core in range(2):
        for half in range(2):
            first = (core * 2 + half) * QUARTER
            mine = wr.at[core, half, x, y]
            for src, dst in (
                (w_in_ref.at[:, pl.ds(D + first, QUARTER)], wq.at[core, half, x, y]),
                (w_in_ref.at[:, pl.ds(first, QUARTER)], mine.at[:, pl.ds(0, QUARTER)]),
                (w_out_ref.at[:, pl.ds(first, QUARTER)], mine.at[:, pl.ds(QUARTER, QUARTER)]),
            ):
                pltpu.make_async_copy(src, dst, load_weights).start()
    load_table = load(table_hbm, table.at[c])
    load_late = [
        load(gain_in_hbm, gain_in_ref),
        load(bias_hbm, bias_ref),
        load(gain_mid_hbm, gain_mid_ref),
        load(counts_hbm, counts_ref),
        load(keys_hbm, keys),
        load(values_hbm, values),
    ]

    for copy in load_small:
        copy.wait()

    chip_row = ((owner_row_ref[...] >> 1) - z) & (PLANES - 1)
    later = lax.broadcasted_iota(jnp.int32, (CAND, CAND), 0)
    earlier = lax.broadcasted_iota(jnp.int32, (CAND, CAND), 1)
    chip_col = jnp.where(earlier == later, chip_row.astype(F32), 0.0)
    chip_col = jnp.sum(chip_col, axis=1, keepdims=True).astype(jnp.int32)
    before = earlier < later
    same = jnp.where((chip_col == chip_row) & before, 1.0, 0.0)
    rank = jnp.sum(same, axis=1, keepdims=True).astype(jnp.int32)
    lane = lax.broadcasted_iota(jnp.int32, (CAND, 128), 1) & 7
    slot_of = jnp.where(lane == rank, 1.0, 0.0).astype(BF16)
    chip_of = chip_row == lax.broadcasted_iota(jnp.int32, (PLANES, CAND), 0)
    row_part = jnp.where(chip_of, row_row_ref[...].astype(F32), 0.0).astype(BF16)
    core_part = jnp.where(chip_of, ((owner_row_ref[...] & 1) + 1).astype(F32), 0.0).astype(BF16)
    wanted = jnp.dot(row_part, slot_of, preferred_element_type=F32)
    wanted += (jnp.dot(core_part, slot_of, preferred_element_type=F32) - 1.0) * ROWS
    wanted = wanted.astype(jnp.int32)
    for step in range(PLANES):
        plan[step] = wanted[step : step + 1]
    asked[0] = wanted[0:1]

    place = chip_col * MESSAGE + rank * PIECES
    column = lax.broadcasted_iota(jnp.int32, (CAND, PLANES * MESSAGE), 1)
    for j in range(PIECES):
        picked = jnp.where(column == place + j, 1.0, 0.0).astype(BF16)
        order[j * CAND : (j + 1) * CAND] = picked

    wait(load_weights, wq.at[0, 0, pl.ds(0, 3)])
    pl.semaphore_wait(barrier, len(peers))

    table_landed = new()
    send(table_hbm, table.at[c], partner, sending(table_hbm), table_landed)
    ask_sent = sending(plan.at[pl.ds(1, PLANES - 1)])
    ask_landed = [new() for _ in GROUPS]
    for step in far_first:
        (index,) = [i for i, steps in enumerate(GROUPS) if PLANES - step in steps]
        send(plan.at[step], asked.at[PLANES - step], at_z(step), ask_sent, ask_landed[index])

    axes = (("y", "x"), ("x", "y"))

    def block(buffer, half, outer, inner):
        if half == 0:
            return buffer.at[c, 0, lax.rem(x + outer, SIDE), lax.rem(y + inner, SIDE)]
        return buffer.at[c, 1, lax.rem(x + inner, SIDE), lax.rem(y + outer, SIDE)]

    def group(buffer, half, outer, first, count):
        if half == 0:
            return buffer.at[c, 0, lax.rem(x + outer, SIDE), pl.ds(first, count)]
        return buffer.at[c, 1, pl.ds(first, count), lax.rem(y + outer, SIDE)]

    def several(buffer, outer):
        return buffer.at[0, :, pl.ds(0, 3)] if outer else buffer.at[0, :, 0, pl.ds(0, 3)]

    class Gather:
        def __init__(self, buffer):
            self.buffer = buffer
            self.two, self.four = buffer.at[0, 0, 0, pl.ds(0, 2)], buffer.at[0, 0, 0]
            self.inner_sent, self.outer_sent = sending(several(buffer, 0)), sending(several(buffer, 1))
            self.share_sent = [sending(several(buffer, 0)), sending(several(buffer, 1))]
            self.share_landed = [new(), new()]
            self.inner_landed = new()
            self.landed = [[new() for _ in range(5)] for _ in range(2)]

        def inner(self):
            for half in range(2):
                mine = block(self.buffer, half, 0, 0)
                for step in (2, 1, 3):
                    send(mine, mine, at_axis(axes[half][0], step), self.inner_sent, self.inner_landed)

        def outer(self):
            wait(self.inner_landed, several(self.buffer, 0))
            for half in range(2):
                for index, (first, step) in enumerate(((0, 1), (2, 3), (2, 1), (0, 3))):
                    part = group(self.buffer, half, 0, first, 2)
                    device = at_axis(axes[half][1], step)
                    send(part, part, device, self.outer_sent, self.landed[half][index])

        def share_inner(self):
            for half in range(2):
                for step in range(1, SIDE):
                    part = block(self.buffer, half, 0, step)
                    send(part, part, partner, self.share_sent[0], self.share_landed[0])

        def relay(self):
            for half in range(2):
                for index, (first, step) in enumerate(((0, 1), (2, 3))):
                    wait(self.landed[half][index], self.two)
                    part = group(self.buffer, half, SIDE - step, first, 2)
                    device = at_axis(axes[half][1], step)
                    send(part, part, device, self.outer_sent, self.landed[half][4])

        def finish(self):
            for half in range(2):
                for index, outer, like in ((2, 3, self.two), (3, 1, self.two), (4, 2, self.four)):
                    wait(self.landed[half][index], like)
                    part = group(self.buffer, half, outer, 0, SIDE)
                    send(part, part, partner, self.share_sent[1], self.share_landed[1])

        def ready(self):
            wait(self.share_landed[0], several(self.buffer, 0))
            wait(self.share_landed[1], several(self.buffer, 1))

    gather_q, gather_r = Gather(wq), Gather(wr)
    gather_q.inner()

    load_table.wait()
    wait(table_landed, table.at[0])
    lanes = lax.broadcasted_iota(jnp.int32, (1, 128), 1)
    items = lax.broadcasted_iota(jnp.int32, (2 * ROWS, 128), 0)
    answer_sent, answer_landed = sending(rows.at[pl.ds(1, PLANES - 1)]), new()

    def serve(index):
        steps = GROUPS[index]
        wait(ask_landed[index], asked.at[pl.ds(1, len([step for step in steps if step]))])
        want = asked[steps[0]]
        for place in range(1, SIDE):
            want = jnp.where(lanes >> 3 == place, asked[steps[place]], want)
        picks = jnp.where((items == want) & (lanes < 32), 1.0, 0.0).astype(BF16)
        found = lax.dot_general(
            picks, table[...].reshape(2 * ROWS, D), (((0,), (0,)), ((), ())), preferred_element_type=F32
        )
        for j in range(PIECES):
            spread[pl.ds(j, 32, stride=PIECES), :] = found[:32, j * 128 : (j + 1) * 128]
        served[index] = spread[...].astype(BF16)
        for place, step in enumerate(steps):
            if step:
                send(
                    served.at[index, pl.ds(place * 64, MESSAGE)],
                    rows.at[PLANES - step],
                    at_z(step),
                    answer_sent,
                    answer_landed,
                )
            else:
                rows[0] = served[index, place * 64 : place * 64 + MESSAGE]

    serve(0)
    serve(1)
    gather_q.outer()
    serve(2)
    serve(3)
    gather_r.inner()
    gather_q.share_inner()
    gather_q.relay()
    gather_r.outer()
    gather_q.finish()
    gather_r.share_inner()

    wait(answer_landed, rows.at[pl.ds(1, PLANES - 1)])
    found = jnp.dot(order[...], rows[...].reshape(PLANES * MESSAGE, 128), preferred_element_type=F32)
    for j in range(PIECES):
        fetched[:, j * 128 : (j + 1) * 128] = found[j * CAND : (j + 1) * CAND].astype(BF16)
    for copy in load_late:
        copy.wait()
    normed[...] = norm(fetched[...].astype(F32), gain_in_ref[...]).astype(BF16)

    gather_r.relay()
    gather_q.ready()

    query_sent = [sending(queries.at[:, 0, pl.ds(0, 3)]), sending(queries.at[:, pl.ds(0, 3)])]
    inner_landed = [{step: new() for step in (2, 1, 3)} for _ in range(2)]
    outer_landed = []
    for half in range(2):
        landed = {key: new() for key in (1, 3, "low", "high")}
        outer_landed.append((landed, {key: new() for key in RELAYED}))

    def send_block(half, place):
        together, alone = outer_landed[half]
        for step in (2, 1, 3) if place == 2 else (1, 3):
            landed = together["high" if step == 2 else step]
            send(
                queries.at[half, 0, place],
                queries.at[half, SIDE - step, place],
                at_axis(axes[half][1], step),
                query_sent[1],
                alone[place, step] if (place, step) in RELAYED else landed,
            )

    def relay_block(half, place, step):
        together, alone = outer_landed[half]
        wait(alone[place, step], queries.at[half, 0, 0])
        send(
            queries.at[half, SIDE - step, place],
            queries.at[half, 2, place],
            at_axis(axes[half][1], step),
            query_sent[1],
            together["low" if place < 2 else "high"],
        )

    for half in range(2):
        for piece in range(2):
            first = D + half * HALF + piece * QUARTER
            projected = jnp.dot(
                normed[...], wq[half, piece].reshape(D, QUARTER), preferred_element_type=F32
            )
            active = silu(projected + bias_ref[:, first : first + QUARTER])
            queries[half, 0, 0, :, piece * QUARTER : (piece + 1) * QUARTER] = active.astype(BF16)
        for step in (2, 1, 3):
            send(
                queries.at[half, 0, 0],
                queries.at[half, 0, SIDE - step],
                at_axis(axes[half][0], step),
                query_sent[0],
                inner_landed[half][step],
            )
        send_block(half, 0)
    for step, place in ((1, 3), (3, 1), (2, 2)):
        for half in range(2):
            wait(inner_landed[half][step], queries.at[half, 0, 0])
            send_block(half, place)

    def attend(half, step, target, first_block=0, count=SIDE):
        blocks = slice(first_block, first_block + count)
        scores = []
        for head in range(HEADS // 2):
            there = slice(head * HEAD, (head + 1) * HEAD)
            first = half * HALF + head * HEAD
            query = queries[half, step, blocks, :, there].reshape(count * CAND, HEAD)
            scores.append(
                lax.dot_general(
                    query,
                    keys[:, first : first + HEAD],
                    (((1,), (1,)), ((), ())),
                    preferred_element_type=F32,
                )
            )
        for head in range(HEADS // 2):
            there = slice(head * HEAD, (head + 1) * HEAD)
            first = half * HALF + head * HEAD
            weights = silu(scores[head], HEAD**-0.5).astype(BF16)
            total = jnp.dot(weights, values[:, first : first + HEAD], preferred_element_type=F32)
            target[blocks, :, there] = total.reshape(count, CAND, HEAD).astype(target.dtype)

    for half in range(2):
        attend(half, 0, own.at[half])

    for place, step in ((0, 1), (3, 3), (1, 1)):
        for half in range(2):
            relay_block(half, place, step)

    part_sent = sending(part_out.at[:, pl.ds(1, 3)])
    part_landed = [new() for _ in range(2)]

    def attend_and_send(half, step, first, count):
        attend(half, step, part_out.at[half, step], first, count)
        blocks = pl.ds(first, count)
        send(
            part_out.at[half, step, blocks],
            part_in.at[half, SIDE - step, blocks],
            at_axis(axes[half][1], step),
            part_sent,
            part_landed[half],
        )

    for step, first, count, key, landed in (
        (3, 0, SIDE, 1, 2),
        (1, 0, SIDE, 3, 3),
        (2, 0, 2, "low", 2),
        (2, 2, 2, "high", 2),
    ):
        for half in range(2):
            wait(outer_landed[half][0][key], queries.at[half, 0, pl.ds(0, landed)])
            attend_and_send(half, step, first, count)

    gather_r.finish()
    gather_r.ready()
    for core in range(2):
        for half in range(2):
            first = (core * 2 + half) * QUARTER
            projected = jnp.dot(
                normed[...],
                wr[core, half, :, :, :, 0:QUARTER].reshape(D, QUARTER),
                preferred_element_type=F32,
            )
            active = silu(projected + bias_ref[:, first : first + QUARTER])
            gates[:, first : first + QUARTER] = active.astype(BF16)

    totals = []
    sum_sent = sending(sum_out.at[:, pl.ds(1, 3)])
    sum_landed = [new() for _ in range(2)]
    for half in range(2):
        wait(part_landed[half], part_in.at[half, pl.ds(1, 3)])

        def summed(place):
            total = own[half, place]
            for step in range(1, SIDE):
                total += part_in[half, step, place].astype(F32)
            return total

        for step in (2, 1, 3):
            sum_out[half, step] = summed(step).astype(BF16)
            send(
                sum_out.at[half, step],
                sum_in.at[half, SIDE - step],
                at_axis(axes[half][0], step),
                sum_sent,
                sum_landed[half],
            )
        totals.append(summed(0))
    attended = []
    for half in range(2):
        wait(sum_landed[half], sum_in.at[half, pl.ds(1, 3)])
        total = totals[half]
        for step in range(1, SIDE):
            total += sum_in[half, step].astype(F32)
        attended.append(total)

    gated = norm(jnp.concatenate(attended, axis=1), gain_mid_ref[...])
    gated = (gated * gates[...].astype(F32)).astype(BF16)
    stores = []
    live = hist * CAND + lax.broadcasted_iota(jnp.int32, (CAND, QUARTER), 0) < counts_ref[...]
    for core in range(2):
        for half in range(2):
            first = (core * 2 + half) * QUARTER
            mixed = jnp.dot(
                gated,
                wr[core, half, :, :, :, QUARTER : 2 * QUARTER].reshape(D, QUARTER),
                preferred_element_type=F32,
            )
            mixed += fetched[:, first : first + QUARTER].astype(F32)
            there = pl.ds(first, QUARTER)
            out_ref[:, there] = jnp.where(live, mixed, 0.0).astype(BF16)
            stores.append(load(out_ref.at[:, there], out_hbm.at[:, there]))

    for semaphore, like in unsent:
        wait(semaphore, like)
    for copy in stores:
        copy.wait()
    assert len(used) == SEMAPHORES, len(used)


def local(
    item_table,
    cand_owner,
    cand_row,
    counts,
    hist_keys,
    hist_values,
    gain_in,
    w_in,
    bias_in,
    gain_mid,
    w_out,
):
    anywhere = pl.BlockSpec(memory_space=pl.ANY)
    events = hist_keys.shape[1]
    result = pl.pallas_call(
        kernel,
        out_shape=jax.ShapeDtypeStruct((CAND, D), BF16),
        in_specs=[anywhere] * 11,
        out_specs=anywhere,
        scratch_shapes=[
            pltpu.VMEM((CAND, D), BF16),
            pltpu.VMEM((1, CAND), jnp.int32),
            pltpu.VMEM((1, CAND), jnp.int32),
            pltpu.VMEM((1, 1), jnp.int32),
            pltpu.VMEM((1, D), F32),
            pltpu.VMEM((1, 2 * D), F32),
            pltpu.VMEM((1, D), F32),
            pltpu.VMEM((2, ROWS, D), BF16),
            pltpu.VMEM((events, D), BF16),
            pltpu.VMEM((events, D), BF16),
            pltpu.VMEM((2, 2, SIDE, SIDE, SHARD, QUARTER), BF16),
            pltpu.VMEM((2, 2, SIDE, SIDE, SHARD, 2 * QUARTER), BF16),
            pltpu.VMEM((PLANES, 1, 128), jnp.int32),
            pltpu.VMEM((PLANES, 1, 128), jnp.int32),
            pltpu.VMEM((PIECES * CAND, PLANES * MESSAGE), BF16),
            pltpu.VMEM((256, 128), F32),
            pltpu.VMEM((len(GROUPS), 256, 128), BF16),
            pltpu.VMEM((PLANES, MESSAGE, 128), BF16),
            pltpu.VMEM((CAND, D), BF16),
            pltpu.VMEM((CAND, D), BF16),
            pltpu.VMEM((CAND, D), BF16),
            pltpu.VMEM((2, SIDE, SIDE, CAND, HALF), BF16),
            pltpu.VMEM((2, SIDE, CAND, HALF), F32),
            pltpu.VMEM((2, SIDE, SIDE, CAND, HALF), BF16),
            pltpu.VMEM((2, SIDE, SIDE, CAND, HALF), BF16),
            pltpu.VMEM((2, SIDE, CAND, HALF), BF16),
            pltpu.VMEM((2, SIDE, CAND, HALF), BF16),
            pltpu.SemaphoreType.DMA((SEMAPHORES,)),
        ],
        compiler_params=pltpu.CompilerParams(
            collective_id=0, has_side_effects=True, vmem_limit_bytes=63 << 20
        ),
        name="layer",
    )(
        item_table,
        cand_owner.reshape(1, CAND),
        cand_row,
        counts.reshape(1, 1),
        hist_keys[0],
        hist_values[0],
        gain_in.reshape(1, D),
        w_in,
        bias_in.reshape(1, 2 * D),
        gain_mid.reshape(1, D),
        w_out,
    )
    return result[None]


def solution(mesh):
    placed = (
        P("users", None),
        P("users", "hist", None),
        P("users", "hist"),
        P("users"),
        P("users", "hist", None),
        P("users", "hist", None),
        P(),
        P("hist", None),
        P(),
        P(),
        P("hist", None),
    )
    return jax.shard_map(
        local, mesh=mesh, in_specs=placed, out_specs=P("users", "hist", None), check_vma=False
    )
```
